256 devices in a mesh: ctx: 128 (over y, x, z), head: 2 (over core).
Axes of the slice: x: 4, y: 4, z: 8, core: 2. Of those that a mesh axis runs over, the one named last changes fastest.
Arguments:
- queries: bfloat16 [32768, 4096], P('ctx', 'head'), parts along dimension 1, may hold values from -3 to 3
- keys: bfloat16 [32768, 256], P('ctx', 'head'), parts along dimension 1, may hold values from -3 to 3
- values: bfloat16 [32768, 256], P('ctx', 'head'), parts along dimension 1, may hold values from -6 to 6
- outputs: bfloat16 [32768, 4096], P('ctx', 'head'), parts along dimension 1, may hold values from -3 to 3
- out_grad: bfloat16 [32768, 4096], P('ctx', 'head'), parts along dimension 1, may hold values from -1.1953125 to 1.1953125
- log_norm: float32 [16, 32768], P(None, 'ctx')
- doc_start: int32 [32768], P('ctx'), may hold values from 0 to 32767, as said below
Outputs:
- query_grad: float32 [32768, 4096], P('ctx', 'head'), parts along dimension 1
- key_grad: float32 [32768, 256], P('ctx', 'head'), parts along dimension 1
- value_grad: float32 [32768, 256], P('ctx', 'head'), parts along dimension 1
The draws below stay inside these ranges and needn't reach their ends.
There are 2 independent parts, one for each index of `head`. The reference program is written for one: setup_inputs(seed, part) draws one part's arguments, and reference() takes and returns one part's arrays. A program takes and returns all parts, laid end to end along the dimension named above; an argument that names none is the same for every part. Nothing has to cross between parts.
Inputs may be any that keep to these rules, and one draw needn't show every extreme that they name: doc_start never falls and doc_start[t] <= t; documents are contiguous and hold at most 1536 tokens, some document exactly that many; the last token begins a document of its own.
All inputs are finite; a program needn't handle non-finite values.
Results may differ from the reference program's by a relative error of at most 0.0045.
Values may be sent and summed in bfloat16 or wider, within the bound.
A program may use at most 64 MiB of HBM per device.

```python
import jax
import jax.numpy as jnp
from jax import lax

HQ = 16
HD = 128
TOK_DEV = 256
REACH = 6
TOKENS = 32768


def document_starts(key):
    longest = REACH * TOK_DEV
    doc_count = TOKENS // (TOK_DEV // 2) + 1
    lengths = jax.random.randint(jax.random.fold_in(key, 101), (doc_count,), TOK_DEV // 2, longest)
    chosen = jax.random.randint(jax.random.fold_in(key, 102), (), 0, 2)
    lengths = jnp.where(jnp.arange(doc_count, dtype=jnp.int32) == chosen, longest, lengths).astype(jnp.int32)
    doc_ends = jnp.cumsum(lengths).astype(jnp.int32)
    beginnings = doc_ends - lengths
    places = jnp.arange(TOKENS, dtype=jnp.int32)
    owner_doc = jnp.sum((doc_ends[None, :] <= places[:, None]).astype(jnp.int32), axis=1)
    starts = jnp.take(beginnings, owner_doc)
    return jnp.where(places == TOKENS - 1, TOKENS - 1, starts).astype(jnp.int32)


def draw_doc_start(key, part):
    starts = document_starts(key)
    return starts


def draw_log_norm(key, part):
    starts = document_starts(key)
    key = jax.random.fold_in(key, 5)
    depth = (jnp.arange(TOKENS, dtype=jnp.int32) - starts + 1).astype(jnp.float32)
    noise = jax.random.uniform(key, (HQ, TOKENS), minval=-0.5, maxval=0.5)
    return (jnp.log(depth)[None, :] + 0.5 + noise).astype(jnp.float32)


def draw_queries(key, part):
    key = jax.random.fold_in(key, 11)
    field = jnp.clip(jax.random.normal(key, (TOKENS, HQ * HD)), -3.0, 3.0)
    return field.astype(jnp.bfloat16)


def draw_keys(key, part):
    key = jax.random.fold_in(key, 13)
    field = jnp.clip(jax.random.normal(key, (TOKENS, HD)), -3.0, 3.0)
    return field.astype(jnp.bfloat16)


def levels(own_key, extent, pieces, smallest, largest):
    def one(axis_at, parts):
        heights = jax.random.uniform(jax.random.fold_in(jax.random.fold_in(own_key, 6), axis_at), (parts,), jnp.float32, smallest / len(pieces), largest / len(pieces))
        return jnp.repeat(jnp.exp(heights), extent[axis_at] // parts).reshape((-1,) + (1,) * (len(extent) - axis_at - 1))

    loudness = one(*pieces[0])
    for cut in pieces[1:]:
        loudness = loudness * one(*cut)
    return loudness


def scatter_about(stream_key, dims, scale, limit, split=(), kind=jnp.bfloat16):
    gain = levels(stream_key, dims, split, -0.22, 0.18) if split else 1.0
    drawn = jax.random.normal(stream_key, dims, jnp.float32) * scale * gain
    return jnp.minimum(jnp.maximum(drawn, -limit), limit).astype(kind)


def setup_inputs(seed: int = 0, part: int = 0) -> dict:
    key_of = jax.random.split(jax.random.key(seed), 8)
    part_splits = jax.random.split(jax.random.fold_in(key_of[7], part), 8)
    return {
        "queries": draw_queries(jax.random.fold_in(jax.random.fold_in(key_of[7], part), 71), part),
        "keys": draw_keys(jax.random.fold_in(jax.random.fold_in(key_of[7], part), 71), part),
        "values": scatter_about(part_splits[2], (TOKENS, HD), 1.0, 6.0, ((0, 128),)),
        "outputs": scatter_about(part_splits[3], (TOKENS, HQ * HD), 0.5, 3.0, ((0, 128),)),
        "out_grad": scatter_about(part_splits[4], (TOKENS, HQ * HD), 0.2, 1.1953125, ((0, 128),)),
        "log_norm": draw_log_norm(jax.random.fold_in(key_of[7], 71), part),
        "doc_start": draw_doc_start(jax.random.fold_in(key_of[7], 71), part),
    }


def reference(queries, keys, values, outputs, out_grad, log_norm, doc_start):
    longest = REACH * TOK_DEV
    window = longest + TOK_DEV
    factor = HD ** -0.5
    products = out_grad.astype(jnp.float32) * outputs.astype(jnp.float32)
    out_dot = jnp.sum(products.reshape(TOKENS, HQ, HD), axis=2).T
    padding = jnp.zeros((longest, HD), jnp.bfloat16)
    keys_padded = jnp.concatenate([padding, keys], axis=0)
    values_padded = jnp.concatenate([padding, values], axis=0)
    starts_all = doc_start.astype(jnp.float32)
    spread = jnp.arange(TOK_DEV, dtype=jnp.int32)
    window_spread = jnp.arange(window, dtype=jnp.int32)

    def visit(totals, block):
        first = (block * TOK_DEV).astype(jnp.int32)
        query_block = lax.dynamic_slice_in_dim(queries, first, TOK_DEV, 0).astype(jnp.float32).reshape(TOK_DEV, HQ, HD)
        grad_block = lax.dynamic_slice_in_dim(out_grad, first, TOK_DEV, 0).astype(jnp.float32).reshape(TOK_DEV, HQ, HD)
        key_block = lax.dynamic_slice_in_dim(keys_padded, first, window, 0).astype(jnp.float32)
        value_block = lax.dynamic_slice_in_dim(values_padded, first, window, 0).astype(jnp.float32)
        norm_block = lax.dynamic_slice_in_dim(log_norm, first, TOK_DEV, 1)
        dot_block = lax.dynamic_slice_in_dim(out_dot, first, TOK_DEV, 1)
        starts = lax.dynamic_slice_in_dim(starts_all, first, TOK_DEV, 0)
        query_spots = (first + spread).astype(jnp.float32)
        key_spots = (first - longest + window_spread).astype(jnp.float32)
        scores = jnp.einsum("thd,kd->htk", query_block, key_block) * factor
        allowed = (key_spots[None, :] >= starts[:, None]) & (key_spots[None, :] <= query_spots[:, None])
        attention = jnp.where(allowed[None], jnp.exp(scores - norm_block[:, :, None]), jnp.float32(0.0))
        rounded = lax.optimization_barrier(attention.astype(jnp.bfloat16)).astype(jnp.float32)
        value_grad = jnp.einsum("htk,thd->kd", rounded, grad_block)
        prob_grad = jnp.einsum("thd,kd->htk", grad_block, value_block)
        score_grad = (attention * (prob_grad - dot_block[:, :, None])).astype(jnp.bfloat16)
        score_grad = lax.optimization_barrier(score_grad).astype(jnp.float32)
        query_grad = jnp.einsum("htk,kd->thd", score_grad, key_block).reshape(TOK_DEV, HQ * HD) * factor
        key_grad = jnp.einsum("htk,thd->kd", score_grad, query_block) * factor
        current = lax.dynamic_slice_in_dim(totals, first, window, 1)
        totals = lax.dynamic_update_slice_in_dim(totals, current + jnp.stack([key_grad, value_grad]), first, 1)
        return totals, query_grad

    totals = jnp.zeros((2, longest + TOKENS, HD), jnp.float32)
    totals, query_grads = lax.scan(visit, totals, jnp.arange(TOKENS // TOK_DEV, dtype=jnp.int32))
    query_grad = query_grads.reshape(TOKENS, HQ * HD)
    return query_grad, totals[0, longest:], totals[1, longest:]
```

```python
import functools

import jax
import jax.numpy as jnp
from jax import lax
from jax.experimental import pallas as pl
from jax.experimental.pallas import tpu as pltpu
from jax.sharding import PartitionSpec as P

MESH = pl.DeviceIdType.MESH
F32 = jnp.float32
BF16 = jnp.bfloat16
REACH = 6
LOG2E = 1.4426950408889634
AHEAD = 2
RELAY = 12


def dot(a, b, ca=1, cb=0):
    return lax.dot_general(a, b, (((ca,), (cb,)), ((), ())), preferred_element_type=F32)


def split(x, parts):
    out = []
    for _ in range(parts):
        piece = x.astype(BF16)
        out.append(piece)
        x = x - piece.astype(F32)
    return out


def kernel(
    n, q_hbm, k_hbm, v_hbm, o_hbm, g_hbm, norm_hbm, start_hbm, dq_hbm, dkv,
    q, g, o, qt, gt, norm, start, lnb, dotb, startb, bias, dq, kv, acc_in, acc_out,
    load_sem, store_sem, key_send, key_recv, acc_send, acc_recv,
):
    rows, width = q.shape
    d = kv.shape[3]
    heads = width // d
    half = rows // 2
    me = lax.axis_index("ctx")

    def at(offset):
        return {"ctx": lax.rem(me + (offset + n), n)}

    loads = [
        pltpu.make_async_copy(src, dst, load_sem.at[i])
        for i, (src, dst) in enumerate(
            [
                (k_hbm, kv.at[REACH, 0]),
                (v_hbm, kv.at[REACH, 1]),
                (norm_hbm, norm),
                (start_hbm, start),
                (q_hbm, q),
                (g_hbm, g),
                (o_hbm, o),
            ]
        )
    ]
    for c in loads:
        c.start()
    barrier = pltpu.get_barrier_semaphore()
    for offset in (1, -1, REACH, -REACH):
        pl.semaphore_signal(barrier, inc=1, device_id=at(offset), device_id_type=MESH)

    dq_store = pltpu.make_async_copy(dq, dq_hbm, store_sem)

    def key_copy(way, src, slot, offset):
        part = pl.ds(way * half, half)
        return pltpu.make_async_remote_copy(
            src_ref=kv.at[src, :, part],
            dst_ref=kv.at[slot, :, part],
            send_sem=key_send.at[way, slot],
            recv_sem=key_recv.at[way, slot],
            device_id=at(offset),
            device_id_type=MESH,
        )

    def acc_copy(way, s, offset):
        return pltpu.make_async_remote_copy(
            src_ref=acc_out.at[way, s],
            dst_ref=acc_in.at[way, s + 1],
            send_sem=acc_send.at[way, s],
            recv_sem=acc_recv.at[way, s + 1],
            device_id=at(offset),
            device_id_type=MESH,
        )

    loads[0].wait()
    loads[1].wait()
    pl.semaphore_wait(barrier, 4)
    key_copy(0, REACH, 0, 1).start()
    key_copy(1, REACH, 0, REACH).start()

    loads[2].wait()
    loads[3].wait()
    pieces = jnp.concatenate(split(norm[...] * LOG2E, 3), axis=0)
    row = lax.broadcasted_iota(jnp.int32, (3 * heads, width), 0)
    col = lax.broadcasted_iota(jnp.int32, (3 * heads, width), 1)
    pick = (col // d == row % heads).astype(F32).astype(BF16)
    lnb[...] = dot(pieces, pick, 0, 0)
    begins = jnp.broadcast_to(start[...].astype(F32), (16, rows))
    coarse = jnp.floor(begins * (1.0 / 256.0)) * 256.0
    line = lax.broadcasted_iota(jnp.int32, (16, rows), 0)
    begins = jnp.where(line == 0, coarse, jnp.where(line == 1, begins - coarse, 0.0))
    startb[...] = dot(begins.astype(BF16), jnp.ones((16, d), BF16), 0, 0)
    loads[4].wait()
    for h in range(heads):
        qt[h] = q[:, h * d : (h + 1) * d].T
    loads[5].wait()
    for h in range(heads):
        gt[h] = g[:, h * d : (h + 1) * d].T
    loads[6].wait()
    ones = jnp.ones((2 * d, d), BF16)
    for h in range(heads):
        cols = slice(h * d, (h + 1) * d)
        product = g[:, cols].astype(F32) * o[:, cols].astype(F32)
        dotb[:, cols] = dot(jnp.concatenate(split(product, 2), axis=1), ones)
    dq[...] = jnp.zeros_like(dq)
    acc_in[0, 0] = jnp.zeros_like(acc_in[0, 0])
    acc_in[1, 0] = jnp.zeros_like(acc_in[1, 0])

    key_copy(0, REACH, 0, 1).wait_recv()
    key_copy(1, REACH, 0, REACH).wait_recv()
    key_copy(0, 0, 1, 1).start()
    key_copy(1, 0, 1, -1).start()

    token = (me * rows).astype(F32) + lax.broadcasted_iota(jnp.int32, (rows, half), 0).astype(F32)
    lane = lax.broadcasted_iota(jnp.int32, (rows, half), 1).astype(F32)

    def step(s, _):
        own = s == REACH
        back = (jnp.where(own, 0, s + 1), REACH - s)
        begin = startb[...]
        for way in range(2):
            spot = ((me - back[way]) * rows + way * half).astype(F32) + lane
            allowed = (spot >= begin) & (spot <= token)
            bias[:, way * half : (way + 1) * half] = jnp.where(allowed, 0.0, -jnp.inf)
        k = kv[s, 0]
        v = kv[s, 1]

        def first(h):
            cols = slice(h * d, (h + 1) * d)
            return dot(q[:, cols], k, 1, 1), dot(g[:, cols], v, 1, 1)

        ready = [first(h) for h in range(AHEAD)]
        dk = jnp.zeros((d, rows), F32)
        dv = jnp.zeros((d, rows), F32)
        for h in range(heads):
            if h == RELAY:

                @pl.when(s < REACH - 1)
                def _():
                    key_copy(0, s, s + 1, 1).wait_recv()
                    key_copy(1, s, s + 1, -1).wait_recv()

                @pl.when(s < REACH - 2)
                def _():
                    key_copy(0, s + 1, s + 2, 1).start()
                    key_copy(1, s + 1, s + 2, -1).start()

            scores, prob_grad = ready.pop(0)
            if h + AHEAD < heads:
                ready.append(first(h + AHEAD))
            cols = slice(h * d, (h + 1) * d)
            shift = lnb[:, cols]
            shift = jnp.concatenate([shift, shift], axis=1)
            minus = dotb[:, cols]
            minus = jnp.concatenate([minus, minus], axis=1)
            attention = jnp.exp2(scores * (d**-0.5 * LOG2E) - shift + bias[...])
            score_grad = (attention * (prob_grad - minus)).astype(BF16)
            dv = dv + dot(gt[h], attention.astype(BF16))
            dk = dk + dot(qt[h], score_grad)
            dq[:, cols] += dot(score_grad, k)
        sums = (dk, dv)

        @pl.when(s == REACH)
        def _():
            dq_store.start()

        @pl.when(s > 0)
        def _():
            acc_copy(0, s - 1, 1).wait_recv()
            acc_copy(1, s - 1, -1).wait_recv()

        for way in range(2):
            cols = slice(way * half, (way + 1) * half)
            for i in range(2):
                total = sums[i][:, cols] + acc_in[way, s, i].astype(F32)
                dkv[i, :, cols] = total
                acc_out[way, s, i] = total.astype(BF16)

        @pl.when(s < REACH - 1)
        def _():
            acc_copy(0, s, 1).start()
            acc_copy(1, s, -1).start()

        @pl.when(s == REACH - 1)
        def _():
            acc_copy(0, s, -REACH).start()
            acc_copy(1, s, -1).start()

        return 0

    lax.fori_loop(0, REACH + 1, step, 0)
    dq_store.wait()

    def drain(s, _):
        for way in range(2):
            key_copy(way, REACH, s, 1).wait_send()
            acc_copy(way, s, 1).wait_send()
        return 0

    lax.fori_loop(0, REACH, drain, 0)


def on_device(n, queries, keys, values, outputs, out_grad, log_norm, doc_start):
    rows, width = queries.shape
    d = keys.shape[1]
    heads = width // d
    half = rows // 2
    anywhere = pl.BlockSpec(memory_space=pl.ANY)
    wide = pltpu.VMEM((rows, width), BF16)
    tall = pltpu.VMEM((heads, d, rows), BF16)
    full = pltpu.VMEM((rows, width), F32)
    copies = pltpu.SemaphoreType.DMA((2, REACH + 1))
    dq, dkv = pl.pallas_call(
        functools.partial(kernel, n),
        out_shape=(
            jax.ShapeDtypeStruct((rows, width), F32),
            jax.ShapeDtypeStruct((2, d, rows), F32),
        ),
        in_specs=[anywhere] * 7,
        out_specs=(anywhere, pl.BlockSpec(memory_space=pltpu.VMEM)),
        scratch_shapes=[
            wide, wide, wide, tall, tall,
            pltpu.VMEM((heads, rows), F32),
            pltpu.VMEM((1, rows), jnp.int32),
            full, full,
            pltpu.VMEM((rows, d), F32),
            pltpu.VMEM((rows, rows), F32),
            full,
            pltpu.VMEM((REACH + 1, 2, rows, d), BF16),
            pltpu.VMEM((2, REACH + 1, 2, d, half), BF16),
            pltpu.VMEM((2, REACH + 1, 2, d, half), BF16),
            pltpu.SemaphoreType.DMA((7,)),
            pltpu.SemaphoreType.DMA,
            copies, copies, copies, copies,
        ],
        compiler_params=pltpu.CompilerParams(
            collective_id=0, has_side_effects=True, vmem_limit_bytes=60 << 20
        ),
    )(queries, keys, values, outputs, out_grad, log_norm, doc_start.reshape(1, rows))
    factor = d**-0.5
    return dq * factor, dkv[0].T * factor, dkv[1].T


def solution(mesh):
    placed = (P("ctx", "head"),) * 5 + (P(None, "ctx"), P("ctx"))
    return jax.shard_map(
        functools.partial(on_device, mesh.shape["ctx"]),
        mesh=mesh,
        in_specs=placed,
        out_specs=(P("ctx", "head"),) * 3,
        check_vma=False,
    )
```

```python
import functools

import jax
import jax.numpy as jnp
from jax import lax
from jax.experimental import pallas as pl
from jax.experimental.pallas import tpu as pltpu
from jax.sharding import PartitionSpec as P

MESH = pl.DeviceIdType.MESH
F32 = jnp.float32
BF16 = jnp.bfloat16
REACH = 6
LOG2E = 1.4426950408889634
AHEAD = 2
RELAY = 12


def dot(a, b, ca=1, cb=0):
    return lax.dot_general(a, b, (((ca,), (cb,)), ((), ())), preferred_element_type=F32)


def split(x, parts):
    out = []
    for _ in range(parts):
        piece = x.astype(BF16)
        out.append(piece)
        x = x - piece.astype(F32)
    return out


def kernel(
    n, q_hbm, k_hbm, v_hbm, o_hbm, g_hbm, norm_hbm, start_hbm, dq_hbm, dkv,
    q, g, o, qt, gt, norm, start, lnb, dotb, startb, bias, dq, kv, acc_in, acc_out,
    load_sem, store_sem, key_send, key_recv, acc_send, acc_recv,
):
    rows, width = q.shape
    d = kv.shape[3]
    heads = width // d
    half = rows // 2
    me = lax.axis_index("ctx")

    def at(offset):
        return {"ctx": lax.rem(me + (offset + n), n)}

    loads = [
        pltpu.make_async_copy(src, dst, load_sem.at[i])
        for i, (src, dst) in enumerate(
            [
                (k_hbm.at[:half], kv.at[REACH, 0, :half]),
                (v_hbm.at[:half], kv.at[REACH, 1, :half]),
                (k_hbm.at[half:], kv.at[0, 0, half:]),
                (v_hbm.at[half:], kv.at[0, 1, half:]),
                (norm_hbm, norm),
                (start_hbm, start),
                (q_hbm, q),
                (g_hbm, g),
                (o_hbm, o),
            ]
        )
    ]
    for c in loads:
        c.start()
    barrier = pltpu.get_barrier_semaphore()
    for offset in (1, -1, REACH, -REACH):
        pl.semaphore_signal(barrier, inc=1, device_id=at(offset), device_id_type=MESH)

    dq_store = pltpu.make_async_copy(dq, dq_hbm, store_sem)

    def key_copy(way, src, slot, offset):
        part = pl.ds(way * half, half)
        return pltpu.make_async_remote_copy(
            src_ref=kv.at[src, :, part],
            dst_ref=kv.at[slot, :, part],
            send_sem=key_send.at[way, slot],
            recv_sem=key_recv.at[way, slot],
            device_id=at(offset),
            device_id_type=MESH,
        )

    def acc_copy(way, s, offset):
        return pltpu.make_async_remote_copy(
            src_ref=acc_out.at[way, s],
            dst_ref=acc_in.at[way, s + 1],
            send_sem=acc_send.at[way, s],
            recv_sem=acc_recv.at[way, s + 1],
            device_id=at(offset),
            device_id_type=MESH,
        )

    for c in loads[:4]:
        c.wait()
    pl.semaphore_wait(barrier, 4)
    key_copy(0, REACH, 0, 1).start()
    key_copy(1, 0, 1, REACH).start()

    loads[4].wait()
    loads[5].wait()
    pieces = jnp.concatenate(split(norm[...] * LOG2E, 3), axis=0)
    row = lax.broadcasted_iota(jnp.int32, (3 * heads, width), 0)
    col = lax.broadcasted_iota(jnp.int32, (3 * heads, width), 1)
    pick = (col // d == row % heads).astype(F32).astype(BF16)
    lnb[...] = dot(pieces, pick, 0, 0)
    begins = jnp.broadcast_to(start[...].astype(F32), (16, rows))
    coarse = jnp.floor(begins * (1.0 / 256.0)) * 256.0
    line = lax.broadcasted_iota(jnp.int32, (16, rows), 0)
    begins = jnp.where(line == 0, coarse, jnp.where(line == 1, begins - coarse, 0.0))
    startb[...] = dot(begins.astype(BF16), jnp.ones((16, d), BF16), 0, 0)
    loads[6].wait()
    for h in range(heads):
        qt[h] = q[:, h * d : (h + 1) * d].T
    loads[7].wait()
    for h in range(heads):
        gt[h] = g[:, h * d : (h + 1) * d].T
    loads[8].wait()
    ones = jnp.ones((2 * d, d), BF16)
    for h in range(heads):
        cols = slice(h * d, (h + 1) * d)
        product = g[:, cols].astype(F32) * o[:, cols].astype(F32)
        dotb[:, cols] = dot(jnp.concatenate(split(product, 2), axis=1), ones)
    dq[...] = jnp.zeros_like(dq)
    for way, slot in ((0, 0), (1, 0), (1, 1)):
        acc_in[way, slot] = jnp.zeros_like(acc_in[way, slot])

    key_copy(0, REACH, 0, 1).wait_recv()
    key_copy(0, 0, 1, 1).start()

    token = (me * rows).astype(F32) + lax.broadcasted_iota(jnp.int32, (rows, half), 0).astype(F32)
    lane = lax.broadcasted_iota(jnp.int32, (rows, half), 1).astype(F32)

    def step(s, _):
        back = (jnp.where(s == REACH, 0, s + 1), jnp.where(s == 0, 0, REACH + 1 - s))
        begin = startb[...]
        for way in range(2):
            spot = ((me - back[way]) * rows + way * half).astype(F32) + lane
            allowed = (spot >= begin) & (spot <= token)
            bias[:, way * half : (way + 1) * half] = jnp.where(allowed, 0.0, -jnp.inf)
        k = kv[s, 0]
        v = kv[s, 1]

        def first(h):
            cols = slice(h * d, (h + 1) * d)
            return dot(q[:, cols], k, 1, 1), dot(g[:, cols], v, 1, 1)

        ready = [first(h) for h in range(AHEAD)]
        dk = jnp.zeros((d, rows), F32)
        dv = jnp.zeros((d, rows), F32)
        for h in range(heads):
            if h == RELAY:

                @pl.when(s < REACH - 1)
                def _():
                    key_copy(0, s, s + 1, 1).wait_recv()

                @pl.when(s < REACH - 2)
                def _():
                    key_copy(0, s + 1, s + 2, 1).start()

                @pl.when(s < REACH)
                def _():
                    key_copy(1, s, s + 1, -1).wait_recv()

                @pl.when(s < REACH - 1)
                def _():
                    key_copy(1, s + 1, s + 2, -1).start()

            scores, prob_grad = ready.pop(0)
            if h + AHEAD < heads:
                ready.append(first(h + AHEAD))
            cols = slice(h * d, (h + 1) * d)
            shift = lnb[:, cols]
            shift = jnp.concatenate([shift, shift], axis=1)
            minus = dotb[:, cols]
            minus = jnp.concatenate([minus, minus], axis=1)
            attention = jnp.exp2(scores * (d**-0.5 * LOG2E) - shift + bias[...])
            score_grad = (attention * (prob_grad - minus)).astype(BF16)
            dv = dv + dot(gt[h], attention.astype(BF16))
            dk = dk + dot(qt[h], score_grad)
            dq[:, cols] += dot(score_grad, k)
        sums = (dk, dv)

        @pl.when(s == REACH)
        def _():
            dq_store.start()

        def finish(way):
            cols = slice(way * half, (way + 1) * half)
            for i in range(2):
                total = sums[i][:, cols] + acc_in[way, s, i].astype(F32)
                acc_out[way, s, i] = total.astype(BF16)
                yield i, cols, total

        @pl.when(s > 0)
        def _():
            acc_copy(0, s - 1, 1).wait_recv()

        for i, cols, total in finish(0):
            dkv[i, :, cols] = total

        @pl.when(s < REACH - 1)
        def _():
            acc_copy(0, s, 1).start()

        @pl.when(s == REACH - 1)
        def _():
            acc_copy(0, s, -REACH).start()

        @pl.when(s > 1)
        def _():
            acc_copy(1, s - 1, -1).wait_recv()

        for i, cols, total in finish(1):

            @pl.when(s == 0)
            def _():
                dkv[i, :, cols] = total

        @pl.when(s > 0)
        def _():
            acc_copy(1, s, -1).start()

        return 0

    lax.fori_loop(0, REACH + 1, step, 0)
    acc_copy(1, REACH, -1).wait_recv()
    dkv[:, :, half:] += acc_in[1, REACH + 1].astype(F32)
    dq_store.wait()

    def drain(s, _):
        for way in range(2):
            key_copy(way, REACH, s + way, 1).wait_send()
            acc_copy(way, s + way, 1).wait_send()
        return 0

    lax.fori_loop(0, REACH, drain, 0)


def finish_kernel(dq_ref, dkv_ref, dq_hbm, dk_hbm, dv_hbm, dq, dk, dv, sems):
    rows, width = dq.shape
    factor = dk.shape[1] ** -0.5
    dk[...] = dkv_ref[0].T * factor
    dv[...] = dkv_ref[1].T
    copies = [
        pltpu.make_async_copy(dk, dk_hbm, sems.at[0]),
        pltpu.make_async_copy(dv, dv_hbm, sems.at[1]),
    ]
    for c in copies:
        c.start()
    part = rows // 4
    for i in range(4):
        here = pl.ds(i * part, part)
        dq[here, :] = dq_ref[here, :] * factor
        copies.append(pltpu.make_async_copy(dq.at[here], dq_hbm.at[here], sems.at[2 + i]))
        copies[-1].start()
    for c in copies:
        c.wait()


def on_device(n, queries, keys, values, outputs, out_grad, log_norm, doc_start):
    rows, width = queries.shape
    d = keys.shape[1]
    heads = width // d
    half = rows // 2
    anywhere = pl.BlockSpec(memory_space=pl.ANY)
    wide = pltpu.VMEM((rows, width), BF16)
    tall = pltpu.VMEM((heads, d, rows), BF16)
    full = pltpu.VMEM((rows, width), F32)
    copies = pltpu.SemaphoreType.DMA((2, REACH + 2))
    dq, dkv = pl.pallas_call(
        functools.partial(kernel, n),
        out_shape=(pltpu.VMEM((rows, width), F32), pltpu.VMEM((2, d, rows), F32)),
        in_specs=[anywhere] * 7,
        out_specs=(anywhere, pl.BlockSpec(memory_space=pltpu.VMEM)),
        scratch_shapes=[
            wide, wide, wide, tall, tall,
            pltpu.VMEM((heads, rows), F32),
            pltpu.VMEM((1, rows), jnp.int32),
            full, full,
            pltpu.VMEM((rows, d), F32),
            pltpu.VMEM((rows, rows), F32),
            full,
            pltpu.VMEM((REACH + 1, 2, rows, d), BF16),
            pltpu.VMEM((2, REACH + 2, 2, d, half), BF16),
            pltpu.VMEM((2, REACH + 1, 2, d, half), BF16),
            pltpu.SemaphoreType.DMA((9,)),
            pltpu.SemaphoreType.DMA,
            copies, copies, copies, copies,
        ],
        compiler_params=pltpu.CompilerParams(
            collective_id=0, has_side_effects=True, vmem_limit_bytes=56 << 20
        ),
    )(queries, keys, values, outputs, out_grad, log_norm, doc_start.reshape(1, rows))
    whole = pl.BlockSpec(memory_space=pltpu.VMEM)
    square = jax.ShapeDtypeStruct((rows, d), F32)
    return pl.pallas_call(
        finish_kernel,
        out_shape=(jax.ShapeDtypeStruct((rows, width), F32), square, square),
        in_specs=[whole, whole],
        out_specs=(anywhere,) * 3,
        scratch_shapes=[
            full,
            pltpu.VMEM((rows, d), F32),
            pltpu.VMEM((rows, d), F32),
            pltpu.SemaphoreType.DMA((6,)),
        ],
        compiler_params=pltpu.CompilerParams(vmem_limit_bytes=16 << 20),
    )(dq, dkv)


def solution(mesh):
    placed = (P("ctx", "head"),) * 5 + (P(None, "ctx"), P("ctx"))
    return jax.shard_map(
        functools.partial(on_device, mesh.shape["ctx"]),
        mesh=mesh,
        in_specs=placed,
        out_specs=(P("ctx", "head"),) * 3,
        check_vma=False,
    )
```

```python
import functools

import jax
import jax.numpy as jnp
from jax import lax
from jax.experimental import pallas as pl
from jax.experimental.pallas import tpu as pltpu
from jax.sharding import PartitionSpec as P

MESH = pl.DeviceIdType.MESH
F32 = jnp.float32
BF16 = jnp.bfloat16
REACH = 6
LOG2E = 1.4426950408889634
AHEAD = 2
RELAY = (12, 12)
LATE = 8


def dot(a, b, ca=1, cb=0):
    return lax.dot_general(a, b, (((ca,), (cb,)), ((), ())), preferred_element_type=F32)


def split(x, parts):
    out = []
    for _ in range(parts):
        piece = x.astype(BF16)
        out.append(piece)
        x = x - piece.astype(F32)
    return out


def kernel(
    n, q_hbm, k_hbm, v_hbm, o_hbm, g_hbm, norm_hbm, start_hbm, dq_hbm, dkv,
    q, g, o, qt, gt, norm, start, lnb, dotb, startb, bias, dq, kv, acc_in, acc_out, later,
    load_sem, store_sem, key_send, key_recv, acc_send, acc_recv,
):
    rows, width = q.shape
    d = kv.shape[4]
    heads = width // d
    half = rows // 2
    me = lax.axis_index("ctx")

    def at(offset):
        return {"ctx": lax.rem(me + (offset + n), n)}

    last = me == n - 1

    @pl.when(me < REACH)
    def _():
        kv[...] = jnp.zeros_like(kv)

    acc_in[...] = jnp.zeros_like(acc_in)
    barrier = pltpu.get_barrier_semaphore()

    peers = jnp.int32(0)

    def greet(offset, meets):
        @pl.when(meets)
        def _():
            pl.semaphore_signal(barrier, inc=1, device_id=at(offset), device_id_type=MESH)

        return jnp.where(meets, 1, 0)

    for offset in (1, -1, REACH, -REACH):
        peers = peers + greet(offset, (me + offset >= 0) & (me + offset < n))
    for offset in range(2, REACH):
        peers = peers + greet(offset, me == n - 1 - offset) + greet(-offset, last)

    loads = [
        pltpu.make_async_copy(src, dst, load_sem.at[i])
        for i, (src, dst) in enumerate(
            [
                (k_hbm.at[:half], kv.at[REACH, 0, 0]),
                (v_hbm.at[:half], kv.at[REACH, 0, 1]),
                (k_hbm.at[half:], kv.at[0, 1, 0]),
                (v_hbm.at[half:], kv.at[0, 1, 1]),
                (norm_hbm, norm),
                (start_hbm, start),
                (q_hbm, q),
                (g_hbm, g),
                (o_hbm, o),
            ]
        )
    ]
    for c in loads:
        c.start()
    dq_store = pltpu.make_async_copy(dq, dq_hbm, store_sem)

    def key_copy(way, src, slot, offset):
        return pltpu.make_async_remote_copy(
            src_ref=kv.at[src, way],
            dst_ref=kv.at[slot, way],
            send_sem=key_send.at[way, slot],
            recv_sem=key_recv.at[way, slot],
            device_id=at(offset),
            device_id_type=MESH,
        )

    def acc_copy(way, s, offset):
        return pltpu.make_async_remote_copy(
            src_ref=acc_out.at[way, s],
            dst_ref=acc_in.at[way, s + 1],
            send_sem=acc_send.at[way, s],
            recv_sem=acc_recv.at[way, s + 1],
            device_id=at(offset),
            device_id_type=MESH,
        )

    def own_send(slot, offset):
        return pltpu.make_async_remote_copy(
            src_ref=kv.at[0, 1],
            dst_ref=kv.at[slot, 1],
            send_sem=key_send.at[1, 0],
            recv_sem=key_recv.at[1, slot],
            device_id=at(offset),
            device_id_type=MESH,
        )

    def acc_home(s):
        return pltpu.make_async_remote_copy(
            src_ref=acc_out.at[0, s],
            dst_ref=acc_in.at[0, REACH],
            send_sem=acc_send.at[0, s],
            recv_sem=acc_recv.at[0, REACH],
            device_id=at(-1 - s),
            device_id_type=MESH,
        )

    for c in loads[:4]:
        c.wait()
    pl.semaphore_wait(barrier, peers)

    @pl.when(me < n - 1)
    def _():
        key_copy(0, REACH, 0, 1).start()

    @pl.when(me < n - REACH)
    def _():
        key_copy(1, 0, 1, REACH).start()

    for offset in range(1, REACH):

        @pl.when(me == n - 1 - offset)
        def _():
            own_send(REACH + 1 - offset, offset).start()

    loads[4].wait()
    loads[5].wait()
    pieces = jnp.concatenate(split(norm[...] * LOG2E, 3), axis=0)
    row = lax.broadcasted_iota(jnp.int32, (3 * heads, width), 0)
    col = lax.broadcasted_iota(jnp.int32, (3 * heads, width), 1)
    pick = (col // d == row % heads).astype(F32).astype(BF16)
    lnb[...] = dot(pieces, pick, 0, 0)
    begins = jnp.broadcast_to(start[...].astype(F32), (16, rows))
    coarse = jnp.floor(begins * (1.0 / 256.0)) * 256.0
    line = lax.broadcasted_iota(jnp.int32, (16, rows), 0)
    begins = jnp.where(line == 0, coarse, jnp.where(line == 1, begins - coarse, 0.0))
    startb[...] = dot(begins.astype(BF16), jnp.ones((16, d), BF16), 0, 0)
    loads[6].wait()
    for h in range(heads):
        qt[h] = q[:, h * d : (h + 1) * d].T
    loads[7].wait()
    for h in range(heads):
        gt[h] = g[:, h * d : (h + 1) * d].T
    loads[8].wait()
    ones = jnp.ones((2 * d, d), BF16)
    for h in range(heads):
        cols = slice(h * d, (h + 1) * d)
        product = g[:, cols].astype(F32) * o[:, cols].astype(F32)
        dotb[:, cols] = dot(jnp.concatenate(split(product, 2), axis=1), ones)
    dq[...] = jnp.zeros_like(dq)

    @pl.when(me > 0)
    def _():
        key_copy(0, REACH, 0, 1).wait_recv()

    @pl.when((me > 0) & (me < n - 1))
    def _():
        key_copy(0, 0, 1, 1).start()

    token = (me * rows).astype(F32) + lax.broadcasted_iota(jnp.int32, (rows, half), 0).astype(F32)
    lane = lax.broadcasted_iota(jnp.int32, (rows, half), 1).astype(F32)

    def pass_on(s):
        @pl.when((s > 1) & (me >= REACH + 1 - s) & (me < n - 1))
        def _():
            acc_copy(1, s - 1, -1).wait_recv()

        acc_out[1, s] = (later[...] + acc_in[1, s].astype(F32)).astype(BF16)

        @pl.when(me >= REACH + 1 - s)
        def _():
            acc_copy(1, s, -1).start()

    def step(s, _):
        back = (jnp.where(s == REACH, 0, s + 1), jnp.where(s == 0, 0, REACH + 1 - s))
        begin = startb[...]
        for way in range(2):
            spot = ((me - back[way]) * rows + way * half).astype(F32) + lane
            allowed = (spot >= begin) & (spot <= token)
            bias[:, way * half : (way + 1) * half] = jnp.where(allowed, 0.0, -jnp.inf)
        k = jnp.concatenate([kv[s, 0, 0], kv[s, 1, 0]], axis=0)
        v = jnp.concatenate([kv[s, 0, 1], kv[s, 1, 1]], axis=0)

        def first(h):
            cols = slice(h * d, (h + 1) * d)
            return dot(q[:, cols], k, 1, 1), dot(g[:, cols], v, 1, 1)

        ready = [first(h) for h in range(AHEAD)]
        dk = jnp.zeros((d, rows), F32)
        dv = jnp.zeros((d, rows), F32)
        for h in range(heads):
            if h == RELAY[0]:

                @pl.when((s < REACH - 1) & (me > s + 1))
                def _():
                    key_copy(0, s, s + 1, 1).wait_recv()

                @pl.when((s < REACH - 2) & (me > s + 1) & (me < n - 1))
                def _():
                    key_copy(0, s + 1, s + 2, 1).start()

            if h == RELAY[1]:

                @pl.when((s < REACH) & (me >= REACH - s))
                def _():
                    key_copy(1, s, s + 1, -1).wait_recv()

                @pl.when((s < REACH - 1) & (me >= REACH - s))
                def _():
                    key_copy(1, s + 1, s + 2, -1).start()

            if h == LATE:

                @pl.when(s > 1)
                def _():
                    pass_on(s - 1)

            scores, prob_grad = ready.pop(0)
            if h + AHEAD < heads:
                ready.append(first(h + AHEAD))
            cols = slice(h * d, (h + 1) * d)
            shift = lnb[:, cols]
            shift = jnp.concatenate([shift, shift], axis=1)
            minus = dotb[:, cols]
            minus = jnp.concatenate([minus, minus], axis=1)
            attention = jnp.exp2(scores * (d**-0.5 * LOG2E) - shift + bias[...])
            score_grad = (attention * (prob_grad - minus)).astype(BF16)
            dv = dv + dot(gt[h], attention.astype(BF16))
            dk = dk + dot(qt[h], score_grad)
            dq[:, cols] += dot(score_grad, k)
        sums = (dk, dv)

        @pl.when(s == REACH)
        def _():
            dq_store.start()

        @pl.when((s > 0) & (((s < REACH) & (me > s)) | ((s == REACH) & (me < n - 1))))
        def _():
            acc_copy(0, s - 1, 1).wait_recv()

        for i in range(2):
            total = sums[i][:, :half] + acc_in[0, s, i].astype(F32)
            dkv[i, :, :half] = total
            acc_out[0, s, i] = total.astype(BF16)
            later[i] = sums[i][:, half:]

        @pl.when((s < REACH - 1) & (me > s) & (me < n - 1))
        def _():
            acc_copy(0, s, 1).start()

        @pl.when((s < REACH) & (me > s) & ((s == REACH - 1) | last))
        def _():
            acc_home(s).start()

        @pl.when(s == 0)
        def _():
            dkv[:, :, half:] = later[...]

        return 0

    lax.fori_loop(0, REACH + 1, step, 0)
    pass_on(jnp.int32(REACH))

    @pl.when(me < n - 1)
    def _():
        acc_copy(1, REACH, -1).wait_recv()

    dkv[:, :, half:] += acc_in[1, REACH + 1].astype(F32)
    dq_store.wait()

    def drain(s, _):
        @pl.when(((s == 0) | (me >= s)) & (me < n - 1))
        def _():
            key_copy(0, REACH, s, 1).wait_send()

        @pl.when(me > s)
        def _():
            acc_copy(0, s, 1).wait_send()

        @pl.when((s > 0) & (me >= REACH + 1 - s))
        def _():
            key_copy(1, REACH, s + 1, 1).wait_send()

        @pl.when(me >= REACH - s)
        def _():
            acc_copy(1, s + 1, 1).wait_send()

        return 0

    @pl.when(me < n - REACH)
    def _():
        key_copy(1, REACH, 1, 1).wait_send()

    for offset in range(1, REACH):

        @pl.when(me == n - 1 - offset)
        def _():
            own_send(REACH + 1 - offset, offset).wait_send()

    lax.fori_loop(0, REACH, drain, 0)


def finish_kernel(dq_ref, dkv_ref, dq_hbm, dk_hbm, dv_hbm, dq, dk, dv, sems):
    rows, width = dq.shape
    factor = dk.shape[1] ** -0.5
    dk[...] = dkv_ref[0].T * factor
    dv[...] = dkv_ref[1].T
    copies = [
        pltpu.make_async_copy(dk, dk_hbm, sems.at[0]),
        pltpu.make_async_copy(dv, dv_hbm, sems.at[1]),
    ]
    for c in copies:
        c.start()
    part = rows // 4
    for i in range(4):
        here = pl.ds(i * part, part)
        dq[here, :] = dq_ref[here, :] * factor
        copies.append(pltpu.make_async_copy(dq.at[here], dq_hbm.at[here], sems.at[2 + i]))
        copies[-1].start()
    for c in copies:
        c.wait()


def on_device(n, queries, keys, values, outputs, out_grad, log_norm, doc_start):
    rows, width = queries.shape
    d = keys.shape[1]
    heads = width // d
    half = rows // 2
    anywhere = pl.BlockSpec(memory_space=pl.ANY)
    wide = pltpu.VMEM((rows, width), BF16)
    tall = pltpu.VMEM((heads, d, rows), BF16)
    full = pltpu.VMEM((rows, width), F32)
    copies = pltpu.SemaphoreType.DMA((2, REACH + 2))
    dq, dkv = pl.pallas_call(
        functools.partial(kernel, n),
        out_shape=(pltpu.VMEM((rows, width), F32), pltpu.VMEM((2, d, rows), F32)),
        in_specs=[anywhere] * 7,
        out_specs=(anywhere, pl.BlockSpec(memory_space=pltpu.VMEM)),
        scratch_shapes=[
            wide, wide, wide, tall, tall,
            pltpu.VMEM((heads, rows), F32),
            pltpu.VMEM((1, rows), jnp.int32),
            full, full,
            pltpu.VMEM((rows, d), F32),
            pltpu.VMEM((rows, rows), F32),
            full,
            pltpu.VMEM((REACH + 1, 2, 2, half, d), BF16),
            pltpu.VMEM((2, REACH + 2, 2, d, half), BF16),
            pltpu.VMEM((2, REACH + 1, 2, d, half), BF16),
            pltpu.VMEM((2, d, half), F32),
            pltpu.SemaphoreType.DMA((9,)),
            pltpu.SemaphoreType.DMA,
            copies, copies, copies, copies,
        ],
        compiler_params=pltpu.CompilerParams(
            collective_id=0, has_side_effects=True, vmem_limit_bytes=56 << 20
        ),
    )(queries, keys, values, outputs, out_grad, log_norm, doc_start.reshape(1, rows))
    whole = pl.BlockSpec(memory_space=pltpu.VMEM)
    square = jax.ShapeDtypeStruct((rows, d), F32)
    return pl.pallas_call(
        finish_kernel,
        out_shape=(jax.ShapeDtypeStruct((rows, width), F32), square, square),
        in_specs=[whole, whole],
        out_specs=(anywhere,) * 3,
        scratch_shapes=[
            full,
            pltpu.VMEM((rows, d), F32),
            pltpu.VMEM((rows, d), F32),
            pltpu.SemaphoreType.DMA((6,)),
        ],
        compiler_params=pltpu.CompilerParams(vmem_limit_bytes=16 << 20),
    )(dq, dkv)


def solution(mesh):
    placed = (P("ctx", "head"),) * 5 + (P(None, "ctx"), P("ctx"))
    return jax.shard_map(
        functools.partial(on_device, mesh.shape["ctx"]),
        mesh=mesh,
        in_specs=placed,
        out_specs=(P("ctx", "head"),) * 3,
        check_vma=False,
    )
```

```python
import functools

import jax
import jax.numpy as jnp
from jax import lax
from jax.experimental import pallas as pl
from jax.experimental.pallas import tpu as pltpu
from jax.sharding import PartitionSpec as P

MESH = pl.DeviceIdType.MESH
F32 = jnp.float32
BF16 = jnp.bfloat16
REACH = 6
LOG2E = 1.4426950408889634
AHEAD = 2
RELAY = (12, 12)
LATE = 8


def dot(a, b, ca=1, cb=0):
    return lax.dot_general(a, b, (((ca,), (cb,)), ((), ())), preferred_element_type=F32)


def split(x, parts):
    out = []
    for _ in range(parts):
        piece = x.astype(BF16)
        out.append(piece)
        x = x - piece.astype(F32)
    return out


def kernel(
    n, q_hbm, k_hbm, v_hbm, o_hbm, g_hbm, norm_hbm, start_hbm, dq_hbm, dkv,
    q, g, o, qt, gt, norm, start, lnb, dotb, startb, bias, dq, kv, acc_in, acc_out, later,
    load_sem, store_sem, key_send, key_recv, acc_send, acc_recv,
):
    rows, width = q.shape
    d = kv.shape[4]
    heads = width // d
    half = rows // 2
    me = lax.axis_index("ctx")

    def at(offset):
        return {"ctx": lax.rem(me + (offset + n), n)}

    last = me == n - 1

    @pl.when(me < REACH)
    def _():
        kv[...] = jnp.zeros_like(kv)

    acc_in[...] = jnp.zeros_like(acc_in)
    barrier = pltpu.get_barrier_semaphore()

    peers = jnp.int32(0)

    def greet(offset, meets):
        @pl.when(meets)
        def _():
            pl.semaphore_signal(barrier, inc=1, device_id=at(offset), device_id_type=MESH)

        return jnp.where(meets, 1, 0)

    for offset in (1, -1, REACH, -REACH):
        peers = peers + greet(offset, (me + offset >= 0) & (me + offset < n))
    for offset in range(2, REACH):
        peers = peers + greet(offset, me == n - 1 - offset) + greet(-offset, last)

    loads = [
        pltpu.make_async_copy(src, dst, load_sem.at[i])
        for i, (src, dst) in enumerate(
            [
                (k_hbm.at[:half], kv.at[REACH, 0, 0]),
                (v_hbm.at[:half], kv.at[REACH, 0, 1]),
                (k_hbm.at[half:], kv.at[0, 1, 0]),
                (v_hbm.at[half:], kv.at[0, 1, 1]),
                (norm_hbm, norm),
                (start_hbm, start),
                (q_hbm, q),
                (g_hbm, g),
                (o_hbm, o),
            ]
        )
    ]
    for c in loads:
        c.start()
    dq_store = pltpu.make_async_copy(dq, dq_hbm, store_sem)

    def key_copy(way, src, slot, offset):
        return pltpu.make_async_remote_copy(
            src_ref=kv.at[src, way],
            dst_ref=kv.at[slot, way],
            send_sem=key_send.at[way, slot],
            recv_sem=key_recv.at[way, slot],
            device_id=at(offset),
            device_id_type=MESH,
        )

    def acc_copy(way, s, offset):
        return pltpu.make_async_remote_copy(
            src_ref=acc_out.at[way, s],
            dst_ref=acc_in.at[way, s + 1],
            send_sem=acc_send.at[way, s],
            recv_sem=acc_recv.at[way, s + 1],
            device_id=at(offset),
            device_id_type=MESH,
        )

    def own_send(slot, offset):
        return pltpu.make_async_remote_copy(
            src_ref=kv.at[0, 1],
            dst_ref=kv.at[slot, 1],
            send_sem=key_send.at[1, 0],
            recv_sem=key_recv.at[1, slot],
            device_id=at(offset),
            device_id_type=MESH,
        )

    def acc_home(s):
        return pltpu.make_async_remote_copy(
            src_ref=acc_out.at[0, s],
            dst_ref=acc_in.at[0, REACH],
            send_sem=acc_send.at[0, s],
            recv_sem=acc_recv.at[0, REACH],
            device_id=at(-1 - s),
            device_id_type=MESH,
        )

    for c in loads[:4]:
        c.wait()
    pl.semaphore_wait(barrier, peers)

    @pl.when(me < n - 1)
    def _():
        key_copy(0, REACH, 0, 1).start()

    @pl.when(me < n - REACH)
    def _():
        key_copy(1, 0, 1, REACH).start()

    for offset in range(1, REACH):

        @pl.when(me == n - 1 - offset)
        def _():
            own_send(REACH + 1 - offset, offset).start()

    loads[4].wait()
    loads[5].wait()
    pieces = jnp.concatenate(split(norm[...] * LOG2E, 3), axis=0)
    row = lax.broadcasted_iota(jnp.int32, (3 * heads, width), 0)
    col = lax.broadcasted_iota(jnp.int32, (3 * heads, width), 1)
    pick = (col // d == row % heads).astype(F32).astype(BF16)
    lnb[...] = dot(pieces, pick, 0, 0)
    begins = jnp.broadcast_to(start[...].astype(F32), (16, rows))
    coarse = jnp.floor(begins * (1.0 / 256.0)) * 256.0
    line = lax.broadcasted_iota(jnp.int32, (16, rows), 0)
    begins = jnp.where(line == 0, coarse, jnp.where(line == 1, begins - coarse, 0.0))
    startb[...] = dot(begins.astype(BF16), jnp.ones((16, d), BF16), 0, 0)
    loads[6].wait()
    for h in range(heads):
        qt[h] = q[:, h * d : (h + 1) * d].T
    loads[7].wait()
    for h in range(heads):
        gt[h] = g[:, h * d : (h + 1) * d].T
    loads[8].wait()
    ones = jnp.ones((2 * d, d), BF16)
    for h in range(heads):
        cols = slice(h * d, (h + 1) * d)
        product = g[:, cols].astype(F32) * o[:, cols].astype(F32)
        dotb[:, cols] = dot(jnp.concatenate(split(product, 2), axis=1), ones)
    dq[...] = jnp.zeros_like(dq)

    @pl.when(me > 0)
    def _():
        key_copy(0, REACH, 0, 1).wait_recv()

    @pl.when((me > 0) & (me < n - 1))
    def _():
        key_copy(0, 0, 1, 1).start()

    token = (me * rows).astype(F32) + lax.broadcasted_iota(jnp.int32, (rows, half), 0).astype(F32)
    lane = lax.broadcasted_iota(jnp.int32, (rows, half), 1).astype(F32)

    def pass_on(s):
        @pl.when((s > 1) & (me >= REACH + 1 - s) & (me < n - 1))
        def _():
            acc_copy(1, s - 1, -1).wait_recv()

        acc_out[1, s] = (later[...] + acc_in[1, s].astype(F32)).astype(BF16)

        @pl.when(me >= REACH + 1 - s)
        def _():
            acc_copy(1, s, -1).start()

    def step(s, _):
        back = (jnp.where(s == REACH, 0, s + 1), jnp.where(s == 0, 0, REACH + 1 - s))
        begin = startb[...]
        for way in range(2):
            spot = ((me - back[way]) * rows + way * half).astype(F32) + lane
            allowed = (spot >= begin) & (spot <= token)
            bias[:, way * half : (way + 1) * half] = jnp.where(allowed, 0.0, -jnp.inf)
        k = jnp.concatenate([kv[s, 0, 0], kv[s, 1, 0]], axis=0)
        v = jnp.concatenate([kv[s, 0, 1], kv[s, 1, 1]], axis=0)

        def first(h):
            cols = slice(h * d, (h + 1) * d)
            return dot(q[:, cols], k, 1, 1), dot(g[:, cols], v, 1, 1)

        ready = [first(h) for h in range(AHEAD)]
        dk = jnp.zeros((d, rows), F32)
        dv = jnp.zeros((d, rows), F32)
        for h in range(heads):
            if h == RELAY[0]:

                @pl.when((s < REACH - 1) & (me > s + 1))
                def _():
                    key_copy(0, s, s + 1, 1).wait_recv()

                @pl.when((s < REACH - 2) & (me > s + 1) & (me < n - 1))
                def _():
                    key_copy(0, s + 1, s + 2, 1).start()

            if h == RELAY[1]:

                @pl.when((s < REACH) & (me >= REACH - s))
                def _():
                    key_copy(1, s, s + 1, -1).wait_recv()

                @pl.when((s < REACH - 1) & (me >= REACH - s))
                def _():
                    key_copy(1, s + 1, s + 2, -1).start()

            if h == LATE:

                @pl.when(s > 1)
                def _():
                    pass_on(s - 1)

            scores, prob_grad = ready.pop(0)
            if h + AHEAD < heads:
                ready.append(first(h + AHEAD))
            cols = slice(h * d, (h + 1) * d)
            shift = lnb[:, cols]
            shift = jnp.concatenate([shift, shift], axis=1)
            minus = dotb[:, cols]
            minus = jnp.concatenate([minus, minus], axis=1)
            attention = jnp.exp2(scores * (d**-0.5 * LOG2E) - shift + bias[...])
            score_grad = (attention * (prob_grad - minus)).astype(BF16)
            dv = dv + dot(gt[h], attention.astype(BF16))
            dk = dk + dot(qt[h], score_grad)
            dq[:, cols] += dot(score_grad, k)
        sums = (dk, dv)

        @pl.when(s == REACH)
        def _():
            dq_store.start()

        @pl.when((s > 0) & (s < REACH) & (me > s))
        def _():
            acc_copy(0, s - 1, 1).wait_recv()

        for i in range(2):
            dkv[i, :, :half] = sums[i][:, :half]
            later[i] = sums[i][:, half:]

        @pl.when(s < REACH)
        def _():
            acc_out[0, s] = (dkv[:, :, :half] + acc_in[0, s].astype(F32)).astype(BF16)

        @pl.when((s < REACH - 1) & (me > s) & (me < n - 1))
        def _():
            acc_copy(0, s, 1).start()

        @pl.when((s < REACH) & (me > s) & ((s == REACH - 1) | last))
        def _():
            acc_home(s).start()

        @pl.when(s == 0)
        def _():
            dkv[:, :, half:] = later[...]

        return 0

    lax.fori_loop(0, REACH + 1, step, 0)
    pass_on(jnp.int32(REACH))

    @pl.when(me < n - 1)
    def _():
        acc_copy(0, REACH - 1, 1).wait_recv()

    dkv[:, :, :half] += acc_in[0, REACH].astype(F32)

    @pl.when(me < n - 1)
    def _():
        acc_copy(1, REACH, -1).wait_recv()

    dkv[:, :, half:] += acc_in[1, REACH + 1].astype(F32)
    dq_store.wait()

    def drain(s, _):
        @pl.when(((s == 0) | (me >= s)) & (me < n - 1))
        def _():
            key_copy(0, REACH, s, 1).wait_send()

        @pl.when(me > s)
        def _():
            acc_copy(0, s, 1).wait_send()

        @pl.when((s > 0) & (me >= REACH + 1 - s))
        def _():
            key_copy(1, REACH, s + 1, 1).wait_send()

        @pl.when(me >= REACH - s)
        def _():
            acc_copy(1, s + 1, 1).wait_send()

        return 0

    @pl.when(me < n - REACH)
    def _():
        key_copy(1, REACH, 1, 1).wait_send()

    for offset in range(1, REACH):

        @pl.when(me == n - 1 - offset)
        def _():
            own_send(REACH + 1 - offset, offset).wait_send()

    lax.fori_loop(0, REACH, drain, 0)


def finish_kernel(dq_ref, dkv_ref, dq_hbm, dk_hbm, dv_hbm, dq, dk, dv, sems):
    rows, width = dq.shape
    factor = dk.shape[1] ** -0.5
    dk[...] = dkv_ref[0].T * factor
    dv[...] = dkv_ref[1].T
    copies = [
        pltpu.make_async_copy(dk, dk_hbm, sems.at[0]),
        pltpu.make_async_copy(dv, dv_hbm, sems.at[1]),
    ]
    for c in copies:
        c.start()
    part = rows // 4
    for i in range(4):
        here = pl.ds(i * part, part)
        dq[here, :] = dq_ref[here, :] * factor
        copies.append(pltpu.make_async_copy(dq.at[here], dq_hbm.at[here], sems.at[2 + i]))
        copies[-1].start()
    for c in copies:
        c.wait()


def on_device(n, queries, keys, values, outputs, out_grad, log_norm, doc_start):
    rows, width = queries.shape
    d = keys.shape[1]
    heads = width // d
    half = rows // 2
    anywhere = pl.BlockSpec(memory_space=pl.ANY)
    wide = pltpu.VMEM((rows, width), BF16)
    tall = pltpu.VMEM((heads, d, rows), BF16)
    full = pltpu.VMEM((rows, width), F32)
    copies = pltpu.SemaphoreType.DMA((2, REACH + 2))
    dq, dkv = pl.pallas_call(
        functools.partial(kernel, n),
        out_shape=(pltpu.VMEM((rows, width), F32), pltpu.VMEM((2, d, rows), F32)),
        in_specs=[anywhere] * 7,
        out_specs=(anywhere, pl.BlockSpec(memory_space=pltpu.VMEM)),
        scratch_shapes=[
            wide, wide, wide, tall, tall,
            pltpu.VMEM((heads, rows), F32),
            pltpu.VMEM((1, rows), jnp.int32),
            full, full,
            pltpu.VMEM((rows, d), F32),
            pltpu.VMEM((rows, rows), F32),
            full,
            pltpu.VMEM((REACH + 1, 2, 2, half, d), BF16),
            pltpu.VMEM((2, REACH + 2, 2, d, half), BF16),
            pltpu.VMEM((2, REACH + 1, 2, d, half), BF16),
            pltpu.VMEM((2, d, half), F32),
            pltpu.SemaphoreType.DMA((9,)),
            pltpu.SemaphoreType.DMA,
            copies, copies, copies, copies,
        ],
        compiler_params=pltpu.CompilerParams(
            collective_id=0, has_side_effects=True, vmem_limit_bytes=56 << 20
        ),
    )(queries, keys, values, outputs, out_grad, log_norm, doc_start.reshape(1, rows))
    whole = pl.BlockSpec(memory_space=pltpu.VMEM)
    square = jax.ShapeDtypeStruct((rows, d), F32)
    return pl.pallas_call(
        finish_kernel,
        out_shape=(jax.ShapeDtypeStruct((rows, width), F32), square, square),
        in_specs=[whole, whole],
        out_specs=(anywhere,) * 3,
        scratch_shapes=[
            full,
            pltpu.VMEM((rows, d), F32),
            pltpu.VMEM((rows, d), F32),
            pltpu.SemaphoreType.DMA((6,)),
        ],
        compiler_params=pltpu.CompilerParams(vmem_limit_bytes=16 << 20),
    )(dq, dkv)


def solution(mesh):
    placed = (P("ctx", "head"),) * 5 + (P(None, "ctx"), P("ctx"))
    return jax.shard_map(
        functools.partial(on_device, mesh.shape["ctx"]),
        mesh=mesh,
        in_specs=placed,
        out_specs=(P("ctx", "head"),) * 3,
        check_vma=False,
    )
```

```python
import functools

import jax
import jax.numpy as jnp
from jax import lax
from jax.experimental import pallas as pl
from jax.experimental.pallas import tpu as pltpu
from jax.sharding import PartitionSpec as P

MESH = pl.DeviceIdType.MESH
F32 = jnp.float32
BF16 = jnp.bfloat16
REACH = 6
LOG2E = 1.4426950408889634
AHEAD = 2
RELAY = (12, 12)
LATE = 8


def dot(a, b, ca=1, cb=0):
    return lax.dot_general(a, b, (((ca,), (cb,)), ((), ())), preferred_element_type=F32)


def split(x, parts):
    out = []
    for _ in range(parts):
        piece = x.astype(BF16)
        out.append(piece)
        x = x - piece.astype(F32)
    return out


def kernel(
    n, q_hbm, k_hbm, v_hbm, o_hbm, g_hbm, norm_hbm, start_hbm, dq_hbm, dkv,
    q, g, o, qt, gt, norm, start, lnb, dotb, startb, bias, dq, kv, acc_in, acc_out, later,
    load_sem, store_sem, key_send, key_recv, acc_send, acc_recv,
):
    rows, width = q.shape
    d = kv.shape[4]
    heads = width // d
    half = rows // 2
    me = lax.axis_index("ctx")

    def at(offset):
        return {"ctx": lax.rem(me + (offset + n), n)}

    last = me == n - 1

    @pl.when(me < REACH)
    def _():
        kv[...] = jnp.zeros_like(kv)

    acc_in[...] = jnp.zeros_like(acc_in)
    barrier = pltpu.get_barrier_semaphore()

    peers = jnp.int32(0)

    def greet(offset, meets):
        @pl.when(meets)
        def _():
            pl.semaphore_signal(barrier, inc=1, device_id=at(offset), device_id_type=MESH)

        return jnp.where(meets, 1, 0)

    for offset in (1, -1, REACH, -REACH):
        peers = peers + greet(offset, (me + offset >= 0) & (me + offset < n))
    for offset in range(2, REACH):
        peers = peers + greet(offset, me == n - 1 - offset) + greet(-offset, last)

    loads = [
        pltpu.make_async_copy(src, dst, load_sem.at[i])
        for i, (src, dst) in enumerate(
            [
                (k_hbm.at[:half], kv.at[REACH, 0, 0]),
                (v_hbm.at[:half], kv.at[REACH, 0, 1]),
                (k_hbm.at[half:], kv.at[0, 1, 0]),
                (v_hbm.at[half:], kv.at[0, 1, 1]),
                (norm_hbm, norm),
                (start_hbm, start),
                (q_hbm, q),
                (g_hbm, g),
                (o_hbm, o),
            ]
        )
    ]
    for c in loads:
        c.start()
    dq_store = pltpu.make_async_copy(dq, dq_hbm, store_sem)

    def key_copy(way, src, slot, offset):
        return pltpu.make_async_remote_copy(
            src_ref=kv.at[src, way],
            dst_ref=kv.at[slot, way],
            send_sem=key_send.at[way, slot],
            recv_sem=key_recv.at[way, slot],
            device_id=at(offset),
            device_id_type=MESH,
        )

    def acc_copy(way, s, offset):
        return pltpu.make_async_remote_copy(
            src_ref=acc_out.at[way, s],
            dst_ref=acc_in.at[way, s + 1],
            send_sem=acc_send.at[way, s],
            recv_sem=acc_recv.at[way, s + 1],
            device_id=at(offset),
            device_id_type=MESH,
        )

    def own_send(slot, offset):
        return pltpu.make_async_remote_copy(
            src_ref=kv.at[0, 1],
            dst_ref=kv.at[slot, 1],
            send_sem=key_send.at[1, 0],
            recv_sem=key_recv.at[1, slot],
            device_id=at(offset),
            device_id_type=MESH,
        )

    def acc_home(s):
        return pltpu.make_async_remote_copy(
            src_ref=acc_out.at[0, s],
            dst_ref=acc_in.at[0, REACH],
            send_sem=acc_send.at[0, s],
            recv_sem=acc_recv.at[0, REACH],
            device_id=at(-1 - s),
            device_id_type=MESH,
        )

    for c in loads[:4]:
        c.wait()
    pl.semaphore_wait(barrier, peers)

    @pl.when(me < n - 1)
    def _():
        key_copy(0, REACH, 0, 1).start()

    @pl.when(me < n - REACH)
    def _():
        key_copy(1, 0, 1, REACH).start()

    for offset in range(1, REACH):

        @pl.when(me == n - 1 - offset)
        def _():
            own_send(REACH + 1 - offset, offset).start()

    loads[4].wait()
    loads[5].wait()
    pieces = jnp.concatenate(split(norm[...] * LOG2E, 3), axis=0)
    row = lax.broadcasted_iota(jnp.int32, (3 * heads, width), 0)
    col = lax.broadcasted_iota(jnp.int32, (3 * heads, width), 1)
    pick = (col // d == row % heads).astype(F32).astype(BF16)
    lnb[...] = dot(pieces, pick, 0, 0)
    begins = jnp.broadcast_to(start[...].astype(F32), (16, rows))
    coarse = jnp.floor(begins * (1.0 / 256.0)) * 256.0
    line = lax.broadcasted_iota(jnp.int32, (16, rows), 0)
    begins = jnp.where(line == 0, coarse, jnp.where(line == 1, begins - coarse, 0.0))
    startb[...] = dot(begins.astype(BF16), jnp.ones((16, d), BF16), 0, 0)
    loads[6].wait()
    for h in range(heads):
        qt[h] = q[:, h * d : (h + 1) * d].T
    loads[7].wait()
    for h in range(heads):
        gt[h] = g[:, h * d : (h + 1) * d].T
    loads[8].wait()
    ones = jnp.ones((2 * d, d), BF16)
    for h in range(heads):
        cols = slice(h * d, (h + 1) * d)
        product = g[:, cols].astype(F32) * o[:, cols].astype(F32)
        dotb[:, cols] = dot(jnp.concatenate(split(product, 2), axis=1), ones)
    dq[...] = jnp.zeros_like(dq)

    @pl.when(me > 0)
    def _():
        key_copy(0, REACH, 0, 1).wait_recv()

    @pl.when((me > 0) & (me < n - 1))
    def _():
        key_copy(0, 0, 1, 1).start()

    token = (me * rows).astype(F32) + lax.broadcasted_iota(jnp.int32, (rows, half), 0).astype(F32)
    lane = lax.broadcasted_iota(jnp.int32, (rows, half), 1).astype(F32)

    def pass_on(s):
        @pl.when((s > 1) & (me >= REACH + 1 - s) & (me < n - 1))
        def _():
            acc_copy(1, s - 1, -1).wait_recv()

        acc_out[1, s] = (later[...] + acc_in[1, s].astype(F32)).astype(BF16)

        @pl.when(me >= REACH + 1 - s)
        def _():
            acc_copy(1, s, -1).start()

    def step(s, _):
        back = (jnp.where(s == REACH, 0, s + 1), jnp.where(s == 0, 0, REACH + 1 - s))
        begin = startb[...]
        for way in range(2):
            spot = ((me - back[way]) * rows + way * half).astype(F32) + lane
            allowed = (spot >= begin) & (spot <= token)
            bias[:, way * half : (way + 1) * half] = jnp.where(allowed, 0.0, -jnp.inf)
        k = jnp.concatenate([kv[s, 0, 0], kv[s, 1, 0]], axis=0)
        v = jnp.concatenate([kv[s, 0, 1], kv[s, 1, 1]], axis=0)

        def first(h):
            cols = slice(h * d, (h + 1) * d)
            return dot(q[:, cols], k, 1, 1), dot(g[:, cols], v, 1, 1)

        ready = [first(h) for h in range(AHEAD)]
        dk = jnp.zeros((d, rows), F32)
        dv = jnp.zeros((d, rows), F32)
        for h in range(heads):
            if h == RELAY[0]:

                @pl.when((s < REACH - 1) & (me > s + 1))
                def _():
                    key_copy(0, s, s + 1, 1).wait_recv()

                @pl.when((s < REACH - 2) & (me > s + 1) & (me < n - 1))
                def _():
                    key_copy(0, s + 1, s + 2, 1).start()

            if h == RELAY[1]:

                @pl.when((s < REACH) & (me >= REACH - s))
                def _():
                    key_copy(1, s, s + 1, -1).wait_recv()

                @pl.when((s < REACH - 1) & (me >= REACH - s))
                def _():
                    key_copy(1, s + 1, s + 2, -1).start()

            if h == LATE:

                @pl.when(s > 1)
                def _():
                    pass_on(s - 1)

            scores, prob_grad = ready.pop(0)
            if h + AHEAD < heads:
                ready.append(first(h + AHEAD))
            cols = slice(h * d, (h + 1) * d)
            shift = lnb[:, cols]
            shift = jnp.concatenate([shift, shift], axis=1)
            minus = dotb[:, cols]
            minus = jnp.concatenate([minus, minus], axis=1)
            attention = jnp.exp2(scores * (d**-0.5 * LOG2E) - shift + bias[...])
            score_grad = (attention * (prob_grad - minus)).astype(BF16)
            dv = dv + dot(gt[h], attention.astype(BF16))
            dk = dk + dot(qt[h], score_grad)
            dq[:, cols] += dot(score_grad, k)
        sums = (dk, dv)

        @pl.when((s > 0) & (s < REACH) & (me > s))
        def _():
            acc_copy(0, s - 1, 1).wait_recv()

        for i in range(2):
            dkv[i, :, :half] = sums[i][:, :half]
            later[i] = sums[i][:, half:]

        @pl.when(s < REACH)
        def _():
            acc_out[0, s] = (dkv[:, :, :half] + acc_in[0, s].astype(F32)).astype(BF16)

        @pl.when((s < REACH - 1) & (me > s) & (me < n - 1))
        def _():
            acc_copy(0, s, 1).start()

        @pl.when((s < REACH) & (me > s) & ((s == REACH - 1) | last))
        def _():
            acc_home(s).start()

        @pl.when(s == 0)
        def _():
            dkv[:, :, half:] = later[...]

        return 0

    lax.fori_loop(0, REACH + 1, step, 0)
    pass_on(jnp.int32(REACH))
    dq[...] = dq[...] * d**-0.5
    dq_store.start()

    @pl.when(me < n - 1)
    def _():
        acc_copy(0, REACH - 1, 1).wait_recv()

    dkv[:, :, :half] += acc_in[0, REACH].astype(F32)

    @pl.when(me < n - 1)
    def _():
        acc_copy(1, REACH, -1).wait_recv()

    dkv[:, :, half:] += acc_in[1, REACH + 1].astype(F32)
    dq_store.wait()

    def drain(s, _):
        @pl.when(((s == 0) | (me >= s)) & (me < n - 1))
        def _():
            key_copy(0, REACH, s, 1).wait_send()

        @pl.when(me > s)
        def _():
            acc_copy(0, s, 1).wait_send()

        @pl.when((s > 0) & (me >= REACH + 1 - s))
        def _():
            key_copy(1, REACH, s + 1, 1).wait_send()

        @pl.when(me >= REACH - s)
        def _():
            acc_copy(1, s + 1, 1).wait_send()

        return 0

    @pl.when(me < n - REACH)
    def _():
        key_copy(1, REACH, 1, 1).wait_send()

    for offset in range(1, REACH):

        @pl.when(me == n - 1 - offset)
        def _():
            own_send(REACH + 1 - offset, offset).wait_send()

    lax.fori_loop(0, REACH, drain, 0)


def finish_kernel(dq_ref, dkv_ref, dq_hbm, dk_hbm, dv_hbm, dk, dv, sems):
    rows = dq_ref.shape[0]
    factor = dk.shape[1] ** -0.5
    part = rows // 4
    copies = []
    for i in range(4):
        here = pl.ds(i * part, part)
        copies.append(pltpu.make_async_copy(dq_ref.at[here], dq_hbm.at[here], sems.at[2 + i]))
        copies[-1].start()
    dk[...] = dkv_ref[0].T * factor
    dv[...] = dkv_ref[1].T
    for i, (src, dst) in enumerate(((dk, dk_hbm), (dv, dv_hbm))):
        copies.append(pltpu.make_async_copy(src, dst, sems.at[i]))
        copies[-1].start()
    for c in copies:
        c.wait()


def on_device(n, queries, keys, values, outputs, out_grad, log_norm, doc_start):
    rows, width = queries.shape
    d = keys.shape[1]
    heads = width // d
    half = rows // 2
    anywhere = pl.BlockSpec(memory_space=pl.ANY)
    wide = pltpu.VMEM((rows, width), BF16)
    tall = pltpu.VMEM((heads, d, rows), BF16)
    full = pltpu.VMEM((rows, width), F32)
    copies = pltpu.SemaphoreType.DMA((2, REACH + 2))
    dq, dkv = pl.pallas_call(
        functools.partial(kernel, n),
        out_shape=(pltpu.VMEM((rows, width), F32), pltpu.VMEM((2, d, rows), F32)),
        in_specs=[anywhere] * 7,
        out_specs=(anywhere, pl.BlockSpec(memory_space=pltpu.VMEM)),
        scratch_shapes=[
            wide, wide, wide, tall, tall,
            pltpu.VMEM((heads, rows), F32),
            pltpu.VMEM((1, rows), jnp.int32),
            full, full,
            pltpu.VMEM((rows, d), F32),
            pltpu.VMEM((rows, rows), F32),
            full,
            pltpu.VMEM((REACH + 1, 2, 2, half, d), BF16),
            pltpu.VMEM((2, REACH + 2, 2, d, half), BF16),
            pltpu.VMEM((2, REACH + 1, 2, d, half), BF16),
            pltpu.VMEM((2, d, half), F32),
            pltpu.SemaphoreType.DMA((9,)),
            pltpu.SemaphoreType.DMA,
            copies, copies, copies, copies,
        ],
        compiler_params=pltpu.CompilerParams(
            collective_id=0, has_side_effects=True, vmem_limit_bytes=56 << 20
        ),
    )(queries, keys, values, outputs, out_grad, log_norm, doc_start.reshape(1, rows))
    whole = pl.BlockSpec(memory_space=pltpu.VMEM)
    square = jax.ShapeDtypeStruct((rows, d), F32)
    return pl.pallas_call(
        finish_kernel,
        out_shape=(jax.ShapeDtypeStruct((rows, width), F32), square, square),
        in_specs=[whole, whole],
        out_specs=(anywhere,) * 3,
        scratch_shapes=[
            pltpu.VMEM((rows, d), F32),
            pltpu.VMEM((rows, d), F32),
            pltpu.SemaphoreType.DMA((6,)),
        ],
        compiler_params=pltpu.CompilerParams(vmem_limit_bytes=16 << 20),
    )(dq, dkv)


def solution(mesh):
    placed = (P("ctx", "head"),) * 5 + (P(None, "ctx"), P("ctx"))
    return jax.shard_map(
        functools.partial(on_device, mesh.shape["ctx"]),
        mesh=mesh,
        in_specs=placed,
        out_specs=(P("ctx", "head"),) * 3,
        check_vma=False,
    )
```
